32 devices in a mesh: dp: 4 (over y, core), section: 2 (over x), tensor: 4 (over z).
Axes of the slice: x: 2, y: 2, z: 4, core: 2. Of those that a mesh axis runs over, the one named last changes fastest.
Arguments:
- saved_input: bfloat16 [2, 2, 512, 8192], P('section', None, ('dp', 'tensor')), may hold values from -6 to 6
- kv_grad: bfloat16 [2, 2, 512, 2048], P('section', None, 'dp', 'tensor'), may hold values from -1.5 to 1.5
- kv_weight: bfloat16 [2, 8192, 2048], P('section', 'dp', 'tensor'), may hold values from -0.0625 to 0.0625
- norm_gain: bfloat16 [2, 8192], P('section'), may hold values from 0.5 to 1.5
- top_grad: bfloat16 [2, 512, 8192], P(None, ('dp', 'tensor')), may hold values from -1.5 to 1.5
- noise_salt: int32 [1], replicated, may hold values from 0 to 1073741823
- step_counter: int32 [1], replicated, may hold values from 0 to 999999
Outputs:
- input_grads: bfloat16 [2, 2, 512, 8192], P('section', None, ('dp', 'tensor'))
- weight_grads: float32 [2, 8192, 2048], P('section', 'dp', 'tensor')
The draws below stay inside these ranges and needn't reach their ends.
All inputs are finite; a program needn't handle non-finite values.
Results may differ from the reference program's by a relative error of at most 0.012.
Values may be sent and summed in bfloat16 or wider, within the bound.
A program may use at most 128 MiB of HBM per device.

```python
import jax
import jax.numpy as jnp
from jax import lax

D = 8192
MB = 2
TOK_DEV = 32
KVW = 2048
LAYERS = 2
TOKENS = 512
N_DP = 4
N_TENSOR = 4


def block_levels(own_key, dims, split, low, high):
    def one(axis_at, shards_of):
        heights = jax.random.uniform(jax.random.fold_in(jax.random.fold_in(own_key, 6), axis_at), (shards_of,), jnp.float32, low / len(split), high / len(split))
        return jnp.repeat(jnp.exp(heights), dims[axis_at] // shards_of).reshape((-1,) + (1,) * (len(dims) - axis_at - 1))

    level = one(*split[0])
    for cut in split[1:]:
        level = level * one(*cut)
    return level


def bell_draw(rng, shape, width, bound, shards=(), held_as=jnp.bfloat16):
    level = block_levels(rng, shape, shards, -0.22, 0.18) if shards else 1.0
    entries = jax.random.normal(rng, shape, jnp.float32) * width * level
    return jnp.minimum(jnp.maximum(entries, -bound), bound).astype(held_as)


def setup_inputs(seed: int = 0) -> dict:
    keys = jax.random.split(jax.random.key(seed), 8)
    return {
        "saved_input": bell_draw(keys[0], (LAYERS, MB, TOKENS, D), 1.0, 6.0, ((0, 2), (2, 16))),
        "kv_grad": bell_draw(keys[1], (LAYERS, MB, TOKENS, KVW), 0.25, 1.5, ((0, 2), (2, 4), (3, 4))),
        "kv_weight": bell_draw(keys[2], (LAYERS, D, KVW), D ** -0.5, 0.0625, ((0, 2), (1, 4), (2, 4))),
        "norm_gain": jnp.clip(1.0 + 0.1 * jax.random.normal(keys[3], (LAYERS, D), jnp.float32), 0.5, 1.5).astype(jnp.bfloat16),
        "top_grad": bell_draw(keys[4], (MB, TOKENS, D), 0.25, 1.5, ((1, 16),)),
        "noise_salt": jax.random.randint(keys[5], (1,), 0, 1073741824).astype(jnp.int32),
        "step_counter": jax.random.randint(keys[6], (1,), 0, 1000000).astype(jnp.int32),
    }


def mix_bits(salt, counter, layer, group, index):
    h = index * jnp.int32(-1640531535) + salt * jnp.int32(374761393) + counter * jnp.int32(668265263)
    h = h + layer * jnp.int32(-1028477379) + group * jnp.int32(1274126177)
    h = h ^ lax.shift_right_logical(h, jnp.int32(16))
    h = h * jnp.int32(2146121005)
    h = h ^ lax.shift_right_logical(h, jnp.int32(15))
    h = h * jnp.int32(-2073254261)
    h = h ^ lax.shift_right_logical(h, jnp.int32(16))
    return lax.shift_right_logical(h, jnp.int32(8)).astype(jnp.float32) * (1.0 / 16777216.0)

def dither(term, salt, counter, layer, group, index):
    noise = mix_bits(salt, counter, layer, group, index)
    moved = term * (1.0 + (noise - 0.5) * 0.5)
    return lax.optimization_barrier(moved.astype(jnp.bfloat16)).astype(jnp.float32)

def reference(saved_input, kv_grad, kv_weight, norm_gain, top_grad, noise_salt, step_counter):
    salt = noise_salt[0]
    counter = step_counter[0]
    width_t = KVW // N_TENSOR
    rows_group = TOK_DEV * N_TENSOR
    top = top_grad.astype(jnp.float32)
    index = jnp.arange(D, dtype=jnp.int32)[:, None] * jnp.int32(KVW) + jnp.arange(KVW, dtype=jnp.int32)[None, :]

    def layer_step(acc, item):
        layer, inputs, cotan, weight, gain = item
        input_float = inputs.astype(jnp.float32)
        inverse_scale = lax.rsqrt(lax.optimization_barrier(jnp.mean(input_float * input_float, axis=-1, keepdims=True)) + 1e-05)
        centered_input = input_float * inverse_scale
        gain_float = gain.astype(jnp.float32)
        normed_values = (centered_input * gain_float).astype(jnp.bfloat16)
        cotanf = cotan.astype(jnp.float32)
        weightf = weight.astype(jnp.float32)
        normed_grad = jnp.zeros((MB, TOKENS, D), jnp.float32)
        for group_t in range(N_TENSOR):
            cols = slice(group_t * width_t, (group_t + 1) * width_t)
            part = jnp.einsum('mtk,dk->mtd', cotanf[:, :, cols], weightf[:, cols])
            normed_grad = normed_grad + part.astype(jnp.bfloat16).astype(jnp.float32)
        hidden_gradient = normed_grad * gain_float
        branch_path = inverse_scale * (hidden_gradient - centered_input * lax.optimization_barrier(jnp.mean(hidden_gradient * centered_input, axis=-1, keepdims=True)))
        acc = acc + branch_path
        grad_in = (top + acc).astype(jnp.bfloat16)
        normedf = normed_values.astype(jnp.float32)
        wsum = jnp.zeros((D, KVW), jnp.float32)
        for group_p in range(N_DP):
            rows = slice(group_p * rows_group, (group_p + 1) * rows_group)
            partial_p = jnp.einsum('mtd,mtk->dk', normedf[:, rows], cotanf[:, rows])
            wsum = wsum + dither(partial_p, salt, counter, layer, jnp.int32(group_p), index)
        return (acc, (grad_in, wsum))
    start = jnp.zeros((MB, TOKENS, D), jnp.float32)
    layers = jnp.arange(LAYERS, dtype=jnp.int32)
    _, outs = lax.scan(layer_step, start, (layers, saved_input, kv_grad, kv_weight, norm_gain), reverse=True)
    return (outs[0], outs[1])
```

```python
import jax
import jax.numpy as jnp
from jax import lax
from jax.sharding import PartitionSpec as P


def entering(shard, axis, join, neutral):
    count = lax.axis_size(axis)
    place = lax.axis_index(axis)
    ahead = count - 1 - place
    gathered = lax.all_gather(shard.astype(jnp.bfloat16), axis)
    state = jnp.zeros_like(shard) + jnp.asarray(neutral, shard.dtype)

    def one(lap, state):
        source = count - 1 - lap
        return join(state, lax.dynamic_index_in_dim(gathered, source, 0, False).astype(shard.dtype))

    return lax.fori_loop(0, ahead, one, state)


def mix_bits(salt, counter, layer, group, index):
    h = (
        index * jnp.int32(-1640531535)
        + salt * jnp.int32(374761393)
        + counter * jnp.int32(668265263)
    )
    h = h + layer * jnp.int32(-1028477379) + group * jnp.int32(1274126177)
    h = h ^ lax.shift_right_logical(h, jnp.int32(16))
    h = h * jnp.int32(2146121005)
    h = h ^ lax.shift_right_logical(h, jnp.int32(15))
    h = h * jnp.int32(-2073254261)
    h = h ^ lax.shift_right_logical(h, jnp.int32(16))
    return lax.shift_right_logical(h, jnp.int32(8)).astype(jnp.float32) * (1.0 / 16777216.0)


def dither(term, salt, counter, layer, group, index):
    noise = mix_bits(salt, counter, layer, group, index)
    moved = term * (1.0 + (noise - 0.5) * 0.5)
    return lax.optimization_barrier(moved.astype(jnp.bfloat16)).astype(jnp.float32)


def add_pair(earlier, later):
    return earlier + later


def shards(saved_input, kv_grad, kv_weight, norm_gain, top_grad, noise_salt, step_counter):
    salt = noise_salt[0]
    counter = step_counter[0]
    layer = lax.axis_index("section")
    group_p = lax.axis_index("dp")
    cotan = kv_grad[0]
    weight = kv_weight[0]
    width_t = weight.shape[1]
    total_cols = width_t * lax.axis_size("tensor")
    col_start = lax.axis_index("tensor") * jnp.int32(width_t)
    input_float = saved_input[0].astype(jnp.float32)
    inverse_scale = lax.rsqrt(jnp.mean(input_float * input_float, axis=-1, keepdims=True) + 1e-05)
    centered_input = input_float * inverse_scale
    gain_float = norm_gain[0].astype(jnp.float32)
    normed_values = (centered_input * gain_float).astype(jnp.bfloat16)
    n_dp = lax.axis_size("dp")
    n_tensor = lax.axis_size("tensor")
    micro, tok, feats = normed_values.shape
    rows = weight.shape[0]
    cotan_all = lax.all_gather(cotan, "dp", axis=0)
    parts = jnp.einsum("pmtk,dk->pmtd", cotan_all, weight, preferred_element_type=jnp.float32)
    mine = lax.psum_scatter(
        parts.astype(jnp.bfloat16), "tensor", scatter_dimension=2, tiled=True
    )
    mine = lax.all_to_all(mine, "dp", split_axis=0, concat_axis=0, tiled=True)
    normed_grad = (
        mine.astype(jnp.float32).transpose(1, 2, 0, 3).reshape(micro, tok, feats)
    )
    sliced = normed_values.reshape(micro, tok, n_dp, rows).transpose(2, 0, 1, 3)
    sliced = lax.all_to_all(sliced, "dp", split_axis=0, concat_axis=0, tiled=True)
    normed_all = lax.all_gather(sliced, "tensor", axis=2, tiled=True)
    hidden_gradient = normed_grad * gain_float
    branch_path = inverse_scale * (
        hidden_gradient
        - centered_input * jnp.mean(hidden_gradient * centered_input, axis=-1, keepdims=True)
    )
    later = entering(branch_path, "section", add_pair, jnp.zeros_like(branch_path))
    grad_in = (top_grad.astype(jnp.float32) + branch_path + later).astype(jnp.bfloat16)
    row_ids = group_p * rows + jnp.arange(rows, dtype=jnp.int32)
    index = (
        row_ids[:, None] * jnp.int32(total_cols)
        + col_start
        + jnp.arange(width_t, dtype=jnp.int32)[None, :]
    )
    wsum = jnp.zeros((rows, width_t), jnp.float32)
    for p in range(n_dp):
        term = jnp.einsum(
            "mtd,mtk->dk", normed_all[p], cotan_all[p], preferred_element_type=jnp.float32
        )
        wsum = wsum + dither(term, salt, counter, layer, jnp.int32(p), index)
    return (grad_in[None], wsum[None])


def solution(mesh):
    placed = (
        P("section", None, ("dp", "tensor"), None),
        P("section", None, "dp", "tensor"),
        P("section", "dp", "tensor"),
        P("section", None),
        P(None, ("dp", "tensor"), None),
        P(),
        P(),
    )
    return jax.shard_map(
        shards,
        mesh=mesh,
        in_specs=placed,
        out_specs=(P("section", None, ("dp", "tensor"), None), P("section", "dp", "tensor")),
        check_vma=False,
    )
```

```python
import functools

import jax
import jax.numpy as jnp
from jax import lax
from jax.experimental import pallas as pl
from jax.experimental.pallas import tpu as pltpu
from jax.sharding import PartitionSpec as P

MESH = pl.DeviceIdType.MESH
F32 = jnp.float32
BF16 = jnp.bfloat16


def kernel(
    n_dp, n_sec, n_t,
    salt_ref, counter_ref, x_ref, kv_ref, w_ref, gain_ref, top_ref,
    out_ref, wout_ref,
    cot, parts, c_right, c_left, norm, nsend, fin, ng, branch, later, relay, scale,
    cot_send, cot_recv, n_send, n_recv, r_send, r_recv, l_send, l_recv,
    g_send, g_recv, s_send, s_recv,
):
    me = lax.axis_index("dp")
    sec = lax.axis_index("section")
    t = lax.axis_index("tensor")
    rows, width = w_ref.shape
    micro, held, _ = kv_ref.shape
    tok = held // n_t
    chunk = micro * tok
    feats = n_dp * rows
    total_cols = width * n_t

    def at(dp=None, section=None, tensor=None):
        return (
            me if dp is None else dp,
            sec if section is None else section,
            t if tensor is None else tensor,
        )

    def peer(k):
        base = lax.rem(me + 2 * (k // 2), n_dp)
        return base + lax.rem(k, 2) * (1 - 2 * lax.rem(base, 2))

    barrier = pltpu.get_barrier_semaphore()

    def greet(where):
        pl.semaphore_signal(barrier, inc=1, device_id=where, device_id_type=MESH)

    for k in range(1, n_dp):
        greet(at(dp=lax.rem(me + k, n_dp)))

    @pl.when(t > 0)
    def _():
        greet(at(tensor=t - 1))

    @pl.when(t < n_t - 1)
    def _():
        greet(at(tensor=t + 1))

    @pl.when(sec > 0)
    def _():
        greet(at(section=sec - 1))

    @pl.when(sec < n_sec - 1)
    def _():
        greet(at(section=sec + 1))

    for j in range(n_t):
        for m in range(micro):
            cot[me, j, m * tok:(m + 1) * tok, :] = kv_ref[m, j * tok:(j + 1) * tok, :]

    greeted = (
        n_dp - 1
        + jnp.where(t > 0, 1, 0) + jnp.where(t < n_t - 1, 1, 0)
        + jnp.where(sec > 0, 1, 0) + jnp.where(sec < n_sec - 1, 1, 0)
    )
    pl.semaphore_wait(barrier, greeted)

    def cot_copy(source, dest):
        return pltpu.make_async_remote_copy(
            src_ref=cot.at[source], dst_ref=cot.at[source],
            send_sem=cot_send.at[dest], recv_sem=cot_recv.at[source],
            device_id=at(dp=dest), device_id_type=MESH,
        )

    def norm_copy(source, dest):
        return pltpu.make_async_remote_copy(
            src_ref=nsend.at[dest], dst_ref=norm.at[source, t],
            send_sem=n_send.at[dest], recv_sem=n_recv.at[source],
            device_id=at(dp=dest), device_id_type=MESH,
        )

    def grad_copy(source, dest):
        return pltpu.make_async_remote_copy(
            src_ref=fin.at[dest], dst_ref=ng.at[source],
            send_sem=g_send.at[dest], recv_sem=g_recv.at[source],
            device_id=at(dp=dest), device_id_type=MESH,
        )

    def section_copy(dest):
        return pltpu.make_async_remote_copy(
            src_ref=relay, dst_ref=later, send_sem=s_send, recv_sem=s_recv,
            device_id=at(section=dest), device_id_type=MESH,
        )

    for k in range(1, n_dp):
        cot_copy(me, peer(k)).start()

    def make_parts(p):
        left = cot[p].reshape(n_t * chunk, width)
        step = min(512, rows)

        @pl.loop(0, rows // step)
        def _(f):
            cols = pl.ds(pl.multiple_of(f * step, step), step)
            got = lax.dot_general(
                left, w_ref[cols, :], (((1,), (1,)), ((), ())), preferred_element_type=F32
            )
            parts[p, :, :, cols] = got.astype(BF16).reshape(n_t, chunk, step)

    make_parts(me)

    def columns(q):
        return slice(q * rows, (q + 1) * rows)

    def normalise():
        total = jnp.zeros((chunk, 1), F32)
        for q in range(n_dp):
            v = x_ref[:, columns(q)].astype(F32)
            total = total + jnp.sum(v * v, axis=-1, keepdims=True)
        r = lax.rsqrt(total * (1.0 / feats) + 1e-05)
        scale[...] = r
        for q in range(n_dp):
            v = x_ref[:, columns(q)].astype(F32) * r
            nsend[q] = (v * gain_ref[:, columns(q)].astype(F32)).astype(BF16)
        norm[me, t] = nsend[me]
        for k in range(1, n_dp):
            norm_copy(me, peer(k)).start()

    def branch_term():
        r = scale[...]
        total = jnp.zeros((chunk, 1), F32)
        for q in range(n_dp):
            h = ng[q].astype(F32) * gain_ref[:, columns(q)].astype(F32)
            xh = x_ref[:, columns(q)].astype(F32) * r
            total = total + jnp.sum(h * xh, axis=-1, keepdims=True)
        mean = total * (1.0 / feats)
        for q in range(n_dp):
            h = ng[q].astype(F32) * gain_ref[:, columns(q)].astype(F32)
            xh = x_ref[:, columns(q)].astype(F32) * r
            branch[:, columns(q)] = r * (h - xh * mean)

    def emit(with_later):
        for q in range(n_dp):
            v = branch[:, columns(q)]
            if with_later:
                v = v + later[:, columns(q)].astype(F32)
            out_ref[:, columns(q)] = (top_ref[:, columns(q)].astype(F32) + v).astype(BF16)
            relay[:, columns(q)] = v.astype(BF16)

    def weight_grad(p, first):
        right = cot[p].reshape(n_t * chunk, width)
        step = min(128, rows)
        base = (
            salt_ref[0] * jnp.int32(374761393)
            + counter_ref[0] * jnp.int32(668265263)
            + sec * jnp.int32(-1028477379)
            + p * jnp.int32(1274126177)
        )
        cell = (
            lax.broadcasted_iota(jnp.int32, (step, width), 0) * jnp.int32(total_cols)
            + lax.broadcasted_iota(jnp.int32, (step, width), 1)
        ) * jnp.int32(-1640531535)

        @pl.loop(0, rows // step)
        def _(f):
            at_rows = pl.ds(pl.multiple_of(f * step, step), step)
            lhs = norm[p, :, :, at_rows].reshape(n_t * chunk, step)
            term = lax.dot_general(
                lhs, right, (((0,), (0,)), ((), ())), preferred_element_type=F32
            )
            origin = (me * rows + f * step) * total_cols + t * width
            h = cell + (base + origin * jnp.int32(-1640531535))
            h = h ^ lax.shift_right_logical(h, jnp.int32(16))
            h = h * jnp.int32(2146121005)
            h = h ^ lax.shift_right_logical(h, jnp.int32(15))
            h = h * jnp.int32(-2073254261)
            h = h ^ lax.shift_right_logical(h, jnp.int32(16))
            u = lax.shift_right_logical(h, jnp.int32(8)).astype(F32) * (1.0 / 16777216.0)
            moved = (term * (1.0 + (u - 0.5) * 0.5)).astype(BF16).astype(F32)
            wout_ref[at_rows, :] = wout_ref[at_rows, :] + moved

    def line_sum(buf, src, p, j, i, send, recv, dest):
        return pltpu.make_async_remote_copy(
            src_ref=src.at[p, j], dst_ref=buf.at[p, j],
            send_sem=send.at[i], recv_sem=recv.at[i],
            device_id=at(tensor=dest), device_id_type=MESH,
        )

    def line_norm(p, j, i, send, recv, dest):
        return pltpu.make_async_remote_copy(
            src_ref=norm.at[p, j], dst_ref=norm.at[p, j],
            send_sem=send.at[i], recv_sem=recv.at[i],
            device_id=at(tensor=dest), device_id_type=MESH,
        )

    sides = (
        (c_right, r_send, r_recv, -1),
        (c_left, l_send, l_recv, 1),
    )

    def each_side(fn, s):
        for buf, send, recv, back in sides:
            if back < 0:
                j, has_in, has_out = n_t - 1 - s, t > 0, t < n_t - 1
                is_sum, lands_sum = j > t, j >= t
            else:
                j, has_in, has_out = s, t < n_t - 1, t > 0
                is_sum, lands_sum = j < t, j <= t
            fn(buf, send, recv, t + back, t - back, j, has_in, has_out, is_sum, lands_sum)

    last_sum = jnp.where((t == 0) | (t == n_t - 1), 0, jnp.maximum(t, n_t - 1 - t))

    def one(i, carry):
        s = i // n_dp
        k = lax.rem(i, n_dp)
        p = peer(k)

        @pl.when((s == 0) & (k > 0))
        def _():
            cot_copy(p, me).wait_recv()
            make_parts(p)

        @pl.when((s == 1) & (k > 0))
        def _():
            norm_copy(p, me).wait_recv()

        def side(buf, send, recv, source, dest, j, has_in, has_out, is_sum, lands_sum):
            @pl.when(has_in & lands_sum)
            def _():
                line_sum(buf, buf, p, j, i, send, recv, source).wait_recv()

            @pl.when(has_in & jnp.logical_not(lands_sum))
            def _():
                line_norm(p, j, i, send, recv, source).wait_recv()

            @pl.when(has_out & is_sum & has_in)
            def _():
                buf[p, j] = (buf[p, j].astype(F32) + parts[p, j].astype(F32)).astype(BF16)
                line_sum(buf, buf, p, j, i, send, recv, dest).start()

            @pl.when(has_out & is_sum & jnp.logical_not(has_in))
            def _():
                line_sum(buf, parts, p, j, i, send, recv, dest).start()

            @pl.when(has_out & jnp.logical_not(is_sum))
            def _():
                line_norm(p, j, i, send, recv, dest).start()

        each_side(side, s)

        @pl.when(i == 0)
        def _():
            normalise()
            wout_ref[...] = jnp.zeros_like(wout_ref)

        @pl.when(s == last_sum)
        def _():
            fin[p] = parts[p, t]

            @pl.when(t > 0)
            def _():
                fin[p] = (fin[p].astype(F32) + c_right[p, t].astype(F32)).astype(BF16)

            @pl.when(t < n_t - 1)
            def _():
                fin[p] = (fin[p].astype(F32) + c_left[p, t].astype(F32)).astype(BF16)

            @pl.when(k == 0)
            def _():
                ng[me] = fin[me]

            @pl.when(k > 0)
            def _():
                grad_copy(me, p).start()

        @pl.when((s == n_t - 1) & (k == min(1, n_dp - 1)))
        def _():
            for kk in range(1, n_dp):
                grad_copy(peer(kk), me).wait_recv()
            branch_term()

            @pl.when(sec == n_sec - 1)
            def _():
                emit(False)

                @pl.when(sec > 0)
                def _():
                    section_copy(sec - 1).start()

        @pl.when(s == n_t - 1)
        def _():
            weight_grad(p, k == 0)

        return carry

    lax.fori_loop(0, n_t * n_dp, one, 0)

    @pl.when(sec < n_sec - 1)
    def _():
        section_copy(sec + 1).wait_recv()
        emit(True)

        @pl.when(sec > 0)
        def _():
            section_copy(sec - 1).start()

    def drain(i, carry):
        s = i // n_dp
        p = peer(lax.rem(i, n_dp))

        def side(buf, send, recv, source, dest, j, has_in, has_out, is_sum, lands_sum):
            @pl.when(has_out & is_sum & has_in)
            def _():
                line_sum(buf, buf, p, j, i, send, recv, dest).wait_send()

            @pl.when(has_out & is_sum & jnp.logical_not(has_in))
            def _():
                line_sum(buf, parts, p, j, i, send, recv, dest).wait_send()

            @pl.when(has_out & jnp.logical_not(is_sum))
            def _():
                line_norm(p, j, i, send, recv, dest).wait_send()

        each_side(side, s)
        return carry

    lax.fori_loop(0, n_t * n_dp, drain, 0)
    for k in range(1, n_dp):
        cot_copy(me, peer(k)).wait_send()
        norm_copy(me, peer(k)).wait_send()
        grad_copy(me, peer(k)).wait_send()

    @pl.when(sec > 0)
    def _():
        section_copy(sec - 1).wait_send()


def shards(saved_input, kv_grad, kv_weight, norm_gain, top_grad, noise_salt, step_counter):
    n_dp, n_sec, n_t = (lax.axis_size(a) for a in ("dp", "section", "tensor"))
    _, micro, tok, feats = saved_input.shape
    rows, width = kv_weight.shape[1:]
    chunk = micro * tok
    vmem = pl.BlockSpec(memory_space=pltpu.VMEM)
    smem = pl.BlockSpec(memory_space=pltpu.SMEM)
    dma = pltpu.SemaphoreType.DMA
    grads, weights = pl.pallas_call(
        functools.partial(kernel, n_dp, n_sec, n_t),
        out_shape=(
            jax.ShapeDtypeStruct((chunk, feats), BF16),
            jax.ShapeDtypeStruct((rows, width), F32),
        ),
        in_specs=[smem, smem] + [vmem] * 5,
        out_specs=(vmem, vmem),
        scratch_shapes=[
            pltpu.VMEM((n_dp, n_t, chunk, width), BF16),
            pltpu.VMEM((n_dp, n_t, chunk, rows), BF16),
            pltpu.VMEM((n_dp, n_t, chunk, rows), BF16),
            pltpu.VMEM((n_dp, n_t, chunk, rows), BF16),
            pltpu.VMEM((n_dp, n_t, chunk, rows), BF16),
            pltpu.VMEM((n_dp, chunk, rows), BF16),
            pltpu.VMEM((n_dp, chunk, rows), BF16),
            pltpu.VMEM((n_dp, chunk, rows), BF16),
            pltpu.VMEM((chunk, feats), F32),
            pltpu.VMEM((chunk, feats), BF16),
            pltpu.VMEM((chunk, feats), BF16),
            pltpu.VMEM((chunk, 1), F32),
            dma((n_dp,)), dma((n_dp,)), dma((n_dp,)), dma((n_dp,)),
            dma((n_t * n_dp,)), dma((n_t * n_dp,)), dma((n_t * n_dp,)), dma((n_t * n_dp,)),
            dma((n_dp,)), dma((n_dp,)), dma, dma,
        ],
        compiler_params=pltpu.CompilerParams(
            collective_id=0, has_side_effects=True, vmem_limit_bytes=56 * 1024 * 1024
        ),
    )(
        noise_salt, step_counter,
        saved_input.reshape(chunk, feats), kv_grad[0], kv_weight[0], norm_gain,
        top_grad.reshape(chunk, feats),
    )
    return grads.reshape(1, micro, tok, feats), weights[None]


def solution(mesh):
    placed = (
        P("section", None, ("dp", "tensor"), None),
        P("section", None, "dp", "tensor"),
        P("section", "dp", "tensor"),
        P("section", None),
        P(None, ("dp", "tensor"), None),
        P(),
        P(),
    )
    return jax.shard_map(
        shards,
        mesh=mesh,
        in_specs=placed,
        out_specs=(P("section", None, ("dp", "tensor"), None), P("section", "dp", "tensor")),
        check_vma=False,
    )
```

```python
import functools

import jax
import jax.numpy as jnp
from jax import lax
from jax.experimental import pallas as pl
from jax.experimental.pallas import tpu as pltpu
from jax.sharding import PartitionSpec as P

MESH = pl.DeviceIdType.MESH
HOP = 2
F32 = jnp.float32
BF16 = jnp.bfloat16


def kernel(
    n_dp, n_sec, n_t,
    salt_ref, counter_ref, x_ref, kv_ref, w_ref, gain_ref, top_ref,
    out_ref, wout_ref,
    cot, parts, c_right, c_left, norm, nsend, fin, ng, branch, later, relay, scale,
    cot_send, cot_recv, n_send, n_recv, r_send, r_recv, l_send, l_recv,
    g_send, g_recv, s_send, s_recv,
):
    me = lax.axis_index("dp")
    sec = lax.axis_index("section")
    t = lax.axis_index("tensor")
    rows, width = w_ref.shape
    micro, held, _ = kv_ref.shape
    tok = held // n_t
    chunk = micro * tok
    feats = n_dp * rows
    total_cols = width * n_t

    def at(dp=None, section=None, tensor=None):
        return (
            me if dp is None else dp,
            sec if section is None else section,
            t if tensor is None else tensor,
        )

    def peer(k):
        base = lax.rem(me + 2 * (k // 2), n_dp)
        return base + lax.rem(k, 2) * (1 - 2 * lax.rem(base, 2))

    barrier = pltpu.get_barrier_semaphore()

    def greet(where):
        pl.semaphore_signal(barrier, inc=1, device_id=where, device_id_type=MESH)

    for k in range(1, n_dp):
        greet(at(dp=lax.rem(me + k, n_dp)))

    @pl.when(t > 0)
    def _():
        greet(at(tensor=t - 1))

    @pl.when(t < n_t - 1)
    def _():
        greet(at(tensor=t + 1))

    @pl.when(sec > 0)
    def _():
        greet(at(section=sec - 1))

    @pl.when(sec < n_sec - 1)
    def _():
        greet(at(section=sec + 1))

    for j in range(n_t):
        for m in range(micro):
            cot[me, j, m * tok:(m + 1) * tok, :] = kv_ref[m, j * tok:(j + 1) * tok, :]

    greeted = (
        n_dp - 1
        + jnp.where(t > 0, 1, 0) + jnp.where(t < n_t - 1, 1, 0)
        + jnp.where(sec > 0, 1, 0) + jnp.where(sec < n_sec - 1, 1, 0)
    )
    pl.semaphore_wait(barrier, greeted)

    def cot_copy(source, dest):
        return pltpu.make_async_remote_copy(
            src_ref=cot.at[source], dst_ref=cot.at[source],
            send_sem=cot_send.at[dest], recv_sem=cot_recv.at[source],
            device_id=at(dp=dest), device_id_type=MESH,
        )

    def norm_copy(source, dest):
        return pltpu.make_async_remote_copy(
            src_ref=nsend.at[dest], dst_ref=norm.at[source, t],
            send_sem=n_send.at[dest], recv_sem=n_recv.at[source],
            device_id=at(dp=dest), device_id_type=MESH,
        )

    def grad_copy(source, dest):
        return pltpu.make_async_remote_copy(
            src_ref=fin.at[dest], dst_ref=ng.at[source],
            send_sem=g_send.at[dest], recv_sem=g_recv.at[source],
            device_id=at(dp=dest), device_id_type=MESH,
        )

    def section_copy(dest):
        return pltpu.make_async_remote_copy(
            src_ref=relay, dst_ref=later, send_sem=s_send, recv_sem=s_recv,
            device_id=at(section=dest), device_id_type=MESH,
        )

    for k in range(1, n_dp):
        cot_copy(me, peer(k)).start()

    def make_parts(p):
        left = cot[p].reshape(n_t * chunk, width)
        step = min(512, rows)

        @pl.loop(0, rows // step)
        def _(f):
            cols = pl.ds(pl.multiple_of(f * step, step), step)
            got = lax.dot_general(
                left, w_ref[cols, :], (((1,), (1,)), ((), ())), preferred_element_type=F32
            )
            parts[p, :, :, cols] = got.astype(BF16).reshape(n_t, chunk, step)

    make_parts(me)

    def columns(q):
        return slice(q * rows, (q + 1) * rows)

    def normalise():
        total = jnp.zeros((chunk, 1), F32)
        for q in range(n_dp):
            v = x_ref[:, columns(q)].astype(F32)
            total = total + jnp.sum(v * v, axis=-1, keepdims=True)
        r = lax.rsqrt(total * (1.0 / feats) + 1e-05)
        scale[...] = r
        for q in range(n_dp):
            v = x_ref[:, columns(q)].astype(F32) * r
            nsend[q] = (v * gain_ref[:, columns(q)].astype(F32)).astype(BF16)
        norm[me, t] = nsend[me]
        for k in range(1, n_dp):
            norm_copy(me, peer(k)).start()

    def branch_term():
        r = scale[...]
        total = jnp.zeros((chunk, 1), F32)
        for q in range(n_dp):
            h = ng[q].astype(F32) * gain_ref[:, columns(q)].astype(F32)
            xh = x_ref[:, columns(q)].astype(F32) * r
            total = total + jnp.sum(h * xh, axis=-1, keepdims=True)
        mean = total * (1.0 / feats)
        for q in range(n_dp):
            h = ng[q].astype(F32) * gain_ref[:, columns(q)].astype(F32)
            xh = x_ref[:, columns(q)].astype(F32) * r
            branch[:, columns(q)] = r * (h - xh * mean)

    def emit(with_later):
        for q in range(n_dp):
            v = branch[:, columns(q)]
            if with_later:
                v = v + later[:, columns(q)].astype(F32)
            out_ref[:, columns(q)] = (top_ref[:, columns(q)].astype(F32) + v).astype(BF16)
            relay[:, columns(q)] = v.astype(BF16)

    def weight_grad(p):
        right = cot[p].reshape(n_t * chunk, width)
        step = min(128, rows)
        base = (
            salt_ref[0] * jnp.int32(374761393)
            + counter_ref[0] * jnp.int32(668265263)
            + sec * jnp.int32(-1028477379)
            + p * jnp.int32(1274126177)
        )
        cell = (
            lax.broadcasted_iota(jnp.int32, (step, width), 0) * jnp.int32(total_cols)
            + lax.broadcasted_iota(jnp.int32, (step, width), 1)
        ) * jnp.int32(-1640531535)

        @pl.loop(0, rows // step)
        def _(f):
            at_rows = pl.ds(pl.multiple_of(f * step, step), step)
            lhs = norm[p, :, :, at_rows].reshape(n_t * chunk, step)
            term = lax.dot_general(
                lhs, right, (((0,), (0,)), ((), ())), preferred_element_type=F32
            )
            origin = (me * rows + f * step) * total_cols + t * width
            h = cell + (base + origin * jnp.int32(-1640531535))
            h = h ^ lax.shift_right_logical(h, jnp.int32(16))
            h = h * jnp.int32(2146121005)
            h = h ^ lax.shift_right_logical(h, jnp.int32(15))
            h = h * jnp.int32(-2073254261)
            h = h ^ lax.shift_right_logical(h, jnp.int32(16))
            u = lax.shift_right_logical(h, jnp.int32(8)).astype(F32) * (1.0 / 16777216.0)
            moved = (term * (1.0 + (u - 0.5) * 0.5)).astype(BF16).astype(F32)
            wout_ref[at_rows, :] = wout_ref[at_rows, :] + moved

    def line_sum(buf, src, p, j, i, send, recv, dest):
        return pltpu.make_async_remote_copy(
            src_ref=src.at[p, j], dst_ref=buf.at[p, j],
            send_sem=send.at[i], recv_sem=recv.at[i],
            device_id=at(tensor=dest), device_id_type=MESH,
        )

    def line_norm(p, j, i, send, recv, dest):
        return pltpu.make_async_remote_copy(
            src_ref=norm.at[p, j], dst_ref=norm.at[p, j],
            send_sem=send.at[i], recv_sem=recv.at[i],
            device_id=at(tensor=dest), device_id_type=MESH,
        )

    sides = (
        (c_right, r_send, r_recv, -1),
        (c_left, l_send, l_recv, 1),
    )

    def turns(fn, c):
        for buf, send, recv, back in sides:
            lag = HOP * t if back < 0 else HOP * (n_t - 1 - t)

            @pl.when((c >= lag) & (c < lag + n_t * n_dp))
            def _():
                i = c - lag
                s = i // n_dp
                p = peer(lax.rem(i, n_dp))
                if back < 0:
                    j, has_in, has_out = n_t - 1 - s, t > 0, t < n_t - 1
                    is_sum, lands_sum = j > t, j >= t
                else:
                    j, has_in, has_out = s, t < n_t - 1, t > 0
                    is_sum, lands_sum = j < t, j <= t
                fn(buf, send, recv, t + back, t - back, j, has_in, has_out, is_sum, lands_sum, p, i)

    total_messages = n_t * n_dp
    sum_turn = jnp.maximum(
        jnp.where(t > 0, (n_t - 1 - t) * n_dp + HOP * t, 0),
        jnp.where(t < n_t - 1, t * n_dp + HOP * (n_t - 1 - t), 0),
    )
    weight_turn = (n_t - 1) * n_dp + HOP * jnp.maximum(t, n_t - 1 - t)

    def one(c, carry):
        @pl.when((c > 0) & (c < n_dp))
        def _():
            cot_copy(peer(c), me).wait_recv()
            make_parts(peer(c))

        @pl.when((c > n_dp) & (c < 2 * n_dp))
        def _():
            norm_copy(peer(c - n_dp), me).wait_recv()

        def side(buf, send, recv, source, dest, j, has_in, has_out, is_sum, lands_sum, p, i):
            @pl.when(has_in & lands_sum)
            def _():
                line_sum(buf, buf, p, j, i, send, recv, source).wait_recv()

            @pl.when(has_in & jnp.logical_not(lands_sum))
            def _():
                line_norm(p, j, i, send, recv, source).wait_recv()

            @pl.when(has_out & is_sum & has_in)
            def _():
                buf[p, j] = (buf[p, j].astype(F32) + parts[p, j].astype(F32)).astype(BF16)
                line_sum(buf, buf, p, j, i, send, recv, dest).start()

            @pl.when(has_out & is_sum & jnp.logical_not(has_in))
            def _():
                line_sum(buf, parts, p, j, i, send, recv, dest).start()

            @pl.when(has_out & jnp.logical_not(is_sum))
            def _():
                line_norm(p, j, i, send, recv, dest).start()

        turns(side, c)

        @pl.when(c == 0)
        def _():
            normalise()
            wout_ref[...] = jnp.zeros_like(wout_ref)

        @pl.when((c >= sum_turn) & (c < sum_turn + n_dp))
        def _():
            k = c - sum_turn
            p = peer(k)
            fin[p] = parts[p, t]

            @pl.when(t > 0)
            def _():
                fin[p] = (fin[p].astype(F32) + c_right[p, t].astype(F32)).astype(BF16)

            @pl.when(t < n_t - 1)
            def _():
                fin[p] = (fin[p].astype(F32) + c_left[p, t].astype(F32)).astype(BF16)

            @pl.when(k == 0)
            def _():
                ng[me] = fin[me]

            @pl.when(k > 0)
            def _():
                grad_copy(me, p).start()

        @pl.when(c == sum_turn + n_dp + 1)
        def _():
            for kk in range(1, n_dp):
                grad_copy(peer(kk), me).wait_recv()
            branch_term()

            @pl.when(sec == n_sec - 1)
            def _():
                emit(False)

                @pl.when(sec > 0)
                def _():
                    section_copy(sec - 1).start()

        @pl.when((c >= weight_turn) & (c < weight_turn + n_dp))
        def _():
            weight_grad(peer(c - weight_turn))

        return carry

    lax.fori_loop(0, total_messages + HOP * (n_t - 1), one, 0)

    @pl.when(sec < n_sec - 1)
    def _():
        section_copy(sec + 1).wait_recv()
        emit(True)

        @pl.when(sec > 0)
        def _():
            section_copy(sec - 1).start()

    def drain(c, carry):
        def side(buf, send, recv, source, dest, j, has_in, has_out, is_sum, lands_sum, p, i):
            @pl.when(has_out & is_sum & has_in)
            def _():
                line_sum(buf, buf, p, j, i, send, recv, dest).wait_send()

            @pl.when(has_out & is_sum & jnp.logical_not(has_in))
            def _():
                line_sum(buf, parts, p, j, i, send, recv, dest).wait_send()

            @pl.when(has_out & jnp.logical_not(is_sum))
            def _():
                line_norm(p, j, i, send, recv, dest).wait_send()

        turns(side, c)
        return carry

    lax.fori_loop(0, total_messages + HOP * (n_t - 1), drain, 0)
    for k in range(1, n_dp):
        cot_copy(me, peer(k)).wait_send()
        norm_copy(me, peer(k)).wait_send()
        grad_copy(me, peer(k)).wait_send()

    @pl.when(sec > 0)
    def _():
        section_copy(sec - 1).wait_send()


def shards(saved_input, kv_grad, kv_weight, norm_gain, top_grad, noise_salt, step_counter):
    n_dp, n_sec, n_t = (lax.axis_size(a) for a in ("dp", "section", "tensor"))
    _, micro, tok, feats = saved_input.shape
    rows, width = kv_weight.shape[1:]
    chunk = micro * tok
    vmem = pl.BlockSpec(memory_space=pltpu.VMEM)
    smem = pl.BlockSpec(memory_space=pltpu.SMEM)
    dma = pltpu.SemaphoreType.DMA
    grads, weights = pl.pallas_call(
        functools.partial(kernel, n_dp, n_sec, n_t),
        out_shape=(
            jax.ShapeDtypeStruct((chunk, feats), BF16),
            jax.ShapeDtypeStruct((rows, width), F32),
        ),
        in_specs=[smem, smem] + [vmem] * 5,
        out_specs=(vmem, vmem),
        scratch_shapes=[
            pltpu.VMEM((n_dp, n_t, chunk, width), BF16),
            pltpu.VMEM((n_dp, n_t, chunk, rows), BF16),
            pltpu.VMEM((n_dp, n_t, chunk, rows), BF16),
            pltpu.VMEM((n_dp, n_t, chunk, rows), BF16),
            pltpu.VMEM((n_dp, n_t, chunk, rows), BF16),
            pltpu.VMEM((n_dp, chunk, rows), BF16),
            pltpu.VMEM((n_dp, chunk, rows), BF16),
            pltpu.VMEM((n_dp, chunk, rows), BF16),
            pltpu.VMEM((chunk, feats), F32),
            pltpu.VMEM((chunk, feats), BF16),
            pltpu.VMEM((chunk, feats), BF16),
            pltpu.VMEM((chunk, 1), F32),
            dma((n_dp,)), dma((n_dp,)), dma((n_dp,)), dma((n_dp,)),
            dma((n_t * n_dp,)), dma((n_t * n_dp,)), dma((n_t * n_dp,)), dma((n_t * n_dp,)),
            dma((n_dp,)), dma((n_dp,)), dma, dma,
        ],
        compiler_params=pltpu.CompilerParams(
            collective_id=0, has_side_effects=True, vmem_limit_bytes=56 * 1024 * 1024
        ),
    )(
        noise_salt, step_counter,
        saved_input.reshape(chunk, feats), kv_grad[0], kv_weight[0], norm_gain,
        top_grad.reshape(chunk, feats),
    )
    return grads.reshape(1, micro, tok, feats), weights[None]


def solution(mesh):
    placed = (
        P("section", None, ("dp", "tensor"), None),
        P("section", None, "dp", "tensor"),
        P("section", "dp", "tensor"),
        P("section", None),
        P(None, ("dp", "tensor"), None),
        P(),
        P(),
    )
    return jax.shard_map(
        shards,
        mesh=mesh,
        in_specs=placed,
        out_specs=(P("section", None, ("dp", "tensor"), None), P("section", "dp", "tensor")),
        check_vma=False,
    )
```

```python
import functools

import jax
import jax.numpy as jnp
from jax import lax
from jax.experimental import pallas as pl
from jax.experimental.pallas import tpu as pltpu
from jax.sharding import PartitionSpec as P

MESH = pl.DeviceIdType.MESH
CUT = 2
HOP = 3
F32 = jnp.float32
BF16 = jnp.bfloat16


def kernel(
    n_dp, n_sec, n_t,
    salt_ref, counter_ref, x_ref, kv_ref, w_ref, gain_ref, top_ref,
    out_ref, wout_ref,
    cot, parts, c_right, c_left, norm, nsend, fin, ng, branch, later, relay, scale,
    cot_send, cot_recv, n_send, n_recv, r_send, r_recv, l_send, l_recv,
    g_send, g_recv, s_send, s_recv,
):
    me = lax.axis_index("dp")
    sec = lax.axis_index("section")
    t = lax.axis_index("tensor")
    rows, width = w_ref.shape
    micro, held, _ = kv_ref.shape
    tok = held // n_t
    chunk = micro * tok
    feats = n_dp * rows
    total_cols = width * n_t

    def at(dp=None, section=None, tensor=None):
        return (
            me if dp is None else dp,
            sec if section is None else section,
            t if tensor is None else tensor,
        )

    def peer(k):
        base = lax.rem(me + 2 * (k // 2), n_dp)
        return base + lax.rem(k, 2) * (1 - 2 * lax.rem(base, 2))

    barrier = pltpu.get_barrier_semaphore()

    def greet(where):
        pl.semaphore_signal(barrier, inc=1, device_id=where, device_id_type=MESH)

    for k in range(1, n_dp):
        greet(at(dp=lax.rem(me + k, n_dp)))

    @pl.when(t > 0)
    def _():
        greet(at(tensor=t - 1))

    @pl.when(t < n_t - 1)
    def _():
        greet(at(tensor=t + 1))

    @pl.when(sec > 0)
    def _():
        greet(at(section=sec - 1))

    @pl.when(sec < n_sec - 1)
    def _():
        greet(at(section=sec + 1))

    for j in range(n_t):
        for m in range(micro):
            cot[me, j, m * tok:(m + 1) * tok, :] = kv_ref[m, j * tok:(j + 1) * tok, :]

    greeted = (
        n_dp - 1
        + jnp.where(t > 0, 1, 0) + jnp.where(t < n_t - 1, 1, 0)
        + jnp.where(sec > 0, 1, 0) + jnp.where(sec < n_sec - 1, 1, 0)
    )
    pl.semaphore_wait(barrier, greeted)

    def cot_copy(source, dest):
        return pltpu.make_async_remote_copy(
            src_ref=cot.at[source], dst_ref=cot.at[source],
            send_sem=cot_send.at[dest], recv_sem=cot_recv.at[source],
            device_id=at(dp=dest), device_id_type=MESH,
        )

    def norm_copy(source, dest):
        return pltpu.make_async_remote_copy(
            src_ref=nsend.at[dest], dst_ref=norm.at[source, t],
            send_sem=n_send.at[dest], recv_sem=n_recv.at[source],
            device_id=at(dp=dest), device_id_type=MESH,
        )

    def grad_copy(source, dest):
        return pltpu.make_async_remote_copy(
            src_ref=fin.at[dest], dst_ref=ng.at[source],
            send_sem=g_send.at[dest], recv_sem=g_recv.at[source],
            device_id=at(dp=dest), device_id_type=MESH,
        )

    def section_copy(dest):
        return pltpu.make_async_remote_copy(
            src_ref=relay, dst_ref=later, send_sem=s_send, recv_sem=s_recv,
            device_id=at(section=dest), device_id_type=MESH,
        )

    for k in range(1, n_dp):
        cot_copy(me, peer(k)).start()

    def make_parts(p):
        left = cot[p].reshape(n_t * chunk, width)
        step = min(512, rows)

        @pl.loop(0, rows // step)
        def _(f):
            cols = pl.ds(pl.multiple_of(f * step, step), step)
            got = lax.dot_general(
                left, w_ref[cols, :], (((1,), (1,)), ((), ())), preferred_element_type=F32
            )
            parts[p, :, :, cols] = got.astype(BF16).reshape(n_t, chunk, step)

    make_parts(me)

    def columns(q):
        return slice(q * rows, (q + 1) * rows)

    def normalise():
        total = jnp.zeros((chunk, 1), F32)
        for q in range(n_dp):
            v = x_ref[:, columns(q)].astype(F32)
            total = total + jnp.sum(v * v, axis=-1, keepdims=True)
        r = lax.rsqrt(total * (1.0 / feats) + 1e-05)
        scale[...] = r
        for q in range(n_dp):
            v = x_ref[:, columns(q)].astype(F32) * r
            nsend[q] = (v * gain_ref[:, columns(q)].astype(F32)).astype(BF16)
        norm[me, t] = nsend[me]
        for k in range(1, n_dp):
            norm_copy(me, peer(k)).start()

    def branch_term():
        r = scale[...]
        total = jnp.zeros((chunk, 1), F32)
        for q in range(n_dp):
            h = ng[q].astype(F32) * gain_ref[:, columns(q)].astype(F32)
            xh = x_ref[:, columns(q)].astype(F32) * r
            total = total + jnp.sum(h * xh, axis=-1, keepdims=True)
        mean = total * (1.0 / feats)
        for q in range(n_dp):
            h = ng[q].astype(F32) * gain_ref[:, columns(q)].astype(F32)
            xh = x_ref[:, columns(q)].astype(F32) * r
            branch[:, columns(q)] = r * (h - xh * mean)

    def emit(with_later):
        for q in range(n_dp):
            v = branch[:, columns(q)]
            if with_later:
                v = v + later[:, columns(q)].astype(F32)
            out_ref[:, columns(q)] = (top_ref[:, columns(q)].astype(F32) + v).astype(BF16)
            relay[:, columns(q)] = v.astype(BF16)

    def weight_grad(p):
        right = cot[p].reshape(n_t * chunk, width)
        step = min(256, rows)
        base = (
            salt_ref[0] * jnp.int32(374761393)
            + counter_ref[0] * jnp.int32(668265263)
            + sec * jnp.int32(-1028477379)
            + p * jnp.int32(1274126177)
        )
        cell = (
            lax.broadcasted_iota(jnp.int32, (step, width), 0) * jnp.int32(total_cols)
            + lax.broadcasted_iota(jnp.int32, (step, width), 1)
        ) * jnp.int32(-1640531535)

        @pl.loop(0, rows // step)
        def _(f):
            at_rows = pl.ds(pl.multiple_of(f * step, step), step)
            lhs = norm[p, :, :, at_rows].reshape(n_t * chunk, step)
            term = lax.dot_general(
                lhs, right, (((0,), (0,)), ((), ())), preferred_element_type=F32
            )
            origin = (me * rows + f * step) * total_cols + t * width
            h = cell + (base + origin * jnp.int32(-1640531535))
            h = h ^ lax.shift_right_logical(h, jnp.int32(16))
            h = h * jnp.int32(2146121005)
            h = h ^ lax.shift_right_logical(h, jnp.int32(15))
            h = h * jnp.int32(-2073254261)
            h = h ^ lax.shift_right_logical(h, jnp.int32(16))
            u = lax.shift_right_logical(h, jnp.int32(8)).astype(F32) * (1.0 / 16777216.0)
            moved = (term * (1.0 + (u - 0.5) * 0.5)).astype(BF16).astype(F32)
            wout_ref[at_rows, :] = wout_ref[at_rows, :] + moved

    part = chunk // CUT
    n_k = n_dp * CUT

    def piece(i):
        return pl.ds(pl.multiple_of(lax.rem(i, CUT) * part, part), part)

    def line_sum(buf, src, p, j, i, send, recv, dest):
        return pltpu.make_async_remote_copy(
            src_ref=src.at[p, j, piece(i)], dst_ref=buf.at[p, j, piece(i)],
            send_sem=send.at[i], recv_sem=recv.at[i],
            device_id=at(tensor=dest), device_id_type=MESH,
        )

    def line_norm(p, j, i, send, recv, dest):
        return pltpu.make_async_remote_copy(
            src_ref=norm.at[p, j, piece(i)], dst_ref=norm.at[p, j, piece(i)],
            send_sem=send.at[i], recv_sem=recv.at[i],
            device_id=at(tensor=dest), device_id_type=MESH,
        )

    sides = (
        (c_right, r_send, r_recv, -1),
        (c_left, l_send, l_recv, 1),
    )

    def turns(fn, c):
        for buf, send, recv, back in sides:
            lag = HOP * t if back < 0 else HOP * (n_t - 1 - t)

            @pl.when((c >= lag) & (c < lag + n_t * n_k))
            def _():
                i = c - lag
                s = i // n_k
                p = peer(lax.rem(i, n_k) // CUT)
                if back < 0:
                    j, has_in, has_out = n_t - 1 - s, t > 0, t < n_t - 1
                    is_sum, lands_sum = j > t, j >= t
                else:
                    j, has_in, has_out = s, t < n_t - 1, t > 0
                    is_sum, lands_sum = j < t, j <= t
                fn(buf, send, recv, t + back, t - back, j, has_in, has_out, is_sum, lands_sum, p, i)

    total_messages = n_t * n_k
    sum_turn = jnp.maximum(
        jnp.where(t > 0, (n_t - 1 - t) * n_k + HOP * t, 0),
        jnp.where(t < n_t - 1, t * n_k + HOP * (n_t - 1 - t), 0),
    )
    weight_turn = (n_t - 1) * n_k + HOP * jnp.maximum(t, n_t - 1 - t)

    def one(c, carry):
        @pl.when((c > 0) & (c < n_k) & (lax.rem(c, CUT) == 0))
        def _():
            cot_copy(peer(c // CUT), me).wait_recv()
            make_parts(peer(c // CUT))

        @pl.when((c > n_k) & (c < 2 * n_k) & (lax.rem(c, CUT) == 0))
        def _():
            norm_copy(peer((c - n_k) // CUT), me).wait_recv()

        def side(buf, send, recv, source, dest, j, has_in, has_out, is_sum, lands_sum, p, i):
            @pl.when(has_in & lands_sum)
            def _():
                line_sum(buf, buf, p, j, i, send, recv, source).wait_recv()

            @pl.when(has_in & jnp.logical_not(lands_sum))
            def _():
                line_norm(p, j, i, send, recv, source).wait_recv()

            @pl.when(has_out & is_sum & has_in)
            def _():
                at_piece = piece(i)
                buf[p, j, at_piece] = (
                    buf[p, j, at_piece].astype(F32) + parts[p, j, at_piece].astype(F32)
                ).astype(BF16)
                line_sum(buf, buf, p, j, i, send, recv, dest).start()

            @pl.when(has_out & is_sum & jnp.logical_not(has_in))
            def _():
                line_sum(buf, parts, p, j, i, send, recv, dest).start()

            @pl.when(has_out & jnp.logical_not(is_sum))
            def _():
                line_norm(p, j, i, send, recv, dest).start()

        turns(side, c)

        @pl.when(c == 0)
        def _():
            normalise()
            wout_ref[...] = jnp.zeros_like(wout_ref)

        @pl.when((c >= sum_turn) & (c < sum_turn + n_k) & (lax.rem(c - sum_turn + CUT * n_k, CUT) == CUT - 1))
        def _():
            k = (c - sum_turn) // CUT
            p = peer(k)
            fin[p] = parts[p, t]

            @pl.when(t > 0)
            def _():
                fin[p] = (fin[p].astype(F32) + c_right[p, t].astype(F32)).astype(BF16)

            @pl.when(t < n_t - 1)
            def _():
                fin[p] = (fin[p].astype(F32) + c_left[p, t].astype(F32)).astype(BF16)

            @pl.when(k == 0)
            def _():
                ng[me] = fin[me]

            @pl.when(k > 0)
            def _():
                grad_copy(me, p).start()

        @pl.when(c == sum_turn + n_k + 2)
        def _():
            for kk in range(1, n_dp):
                grad_copy(peer(kk), me).wait_recv()
            branch_term()

            @pl.when(sec == n_sec - 1)
            def _():
                emit(False)

                @pl.when(sec > 0)
                def _():
                    section_copy(sec - 1).start()

        @pl.when((c >= weight_turn) & (c < weight_turn + n_k) & (lax.rem(c - weight_turn + 2 * total_messages, CUT) == CUT - 1))
        def _():
            weight_grad(peer((c - weight_turn) // CUT))

        return carry

    lax.fori_loop(0, total_messages + HOP * (n_t - 1), one, 0)

    @pl.when(sec < n_sec - 1)
    def _():
        section_copy(sec + 1).wait_recv()
        emit(True)

        @pl.when(sec > 0)
        def _():
            section_copy(sec - 1).start()

    def drain(c, carry):
        def side(buf, send, recv, source, dest, j, has_in, has_out, is_sum, lands_sum, p, i):
            @pl.when(has_out & is_sum & has_in)
            def _():
                line_sum(buf, buf, p, j, i, send, recv, dest).wait_send()

            @pl.when(has_out & is_sum & jnp.logical_not(has_in))
            def _():
                line_sum(buf, parts, p, j, i, send, recv, dest).wait_send()

            @pl.when(has_out & jnp.logical_not(is_sum))
            def _():
                line_norm(p, j, i, send, recv, dest).wait_send()

        turns(side, c)
        return carry

    lax.fori_loop(0, total_messages + HOP * (n_t - 1), drain, 0)
    for k in range(1, n_dp):
        cot_copy(me, peer(k)).wait_send()
        norm_copy(me, peer(k)).wait_send()
        grad_copy(me, peer(k)).wait_send()

    @pl.when(sec > 0)
    def _():
        section_copy(sec - 1).wait_send()


def shards(saved_input, kv_grad, kv_weight, norm_gain, top_grad, noise_salt, step_counter):
    n_dp, n_sec, n_t = (lax.axis_size(a) for a in ("dp", "section", "tensor"))
    _, micro, tok, feats = saved_input.shape
    rows, width = kv_weight.shape[1:]
    chunk = micro * tok
    vmem = pl.BlockSpec(memory_space=pltpu.VMEM)
    smem = pl.BlockSpec(memory_space=pltpu.SMEM)
    dma = pltpu.SemaphoreType.DMA
    grads, weights = pl.pallas_call(
        functools.partial(kernel, n_dp, n_sec, n_t),
        out_shape=(
            jax.ShapeDtypeStruct((chunk, feats), BF16),
            jax.ShapeDtypeStruct((rows, width), F32),
        ),
        in_specs=[smem, smem] + [vmem] * 5,
        out_specs=(vmem, vmem),
        scratch_shapes=[
            pltpu.VMEM((n_dp, n_t, chunk, width), BF16),
            pltpu.VMEM((n_dp, n_t, chunk, rows), BF16),
            pltpu.VMEM((n_dp, n_t, chunk, rows), BF16),
            pltpu.VMEM((n_dp, n_t, chunk, rows), BF16),
            pltpu.VMEM((n_dp, n_t, chunk, rows), BF16),
            pltpu.VMEM((n_dp, chunk, rows), BF16),
            pltpu.VMEM((n_dp, chunk, rows), BF16),
            pltpu.VMEM((n_dp, chunk, rows), BF16),
            pltpu.VMEM((chunk, feats), F32),
            pltpu.VMEM((chunk, feats), BF16),
            pltpu.VMEM((chunk, feats), BF16),
            pltpu.VMEM((chunk, 1), F32),
            dma((n_dp,)), dma((n_dp,)), dma((n_dp,)), dma((n_dp,)),
            dma((n_t * n_dp * CUT,)), dma((n_t * n_dp * CUT,)), dma((n_t * n_dp * CUT,)), dma((n_t * n_dp * CUT,)),
            dma((n_dp,)), dma((n_dp,)), dma, dma,
        ],
        compiler_params=pltpu.CompilerParams(
            collective_id=0, has_side_effects=True, vmem_limit_bytes=56 * 1024 * 1024
        ),
    )(
        noise_salt, step_counter,
        saved_input.reshape(chunk, feats), kv_grad[0], kv_weight[0], norm_gain,
        top_grad.reshape(chunk, feats),
    )
    return grads.reshape(1, micro, tok, feats), weights[None]


def solution(mesh):
    placed = (
        P("section", None, ("dp", "tensor"), None),
        P("section", None, "dp", "tensor"),
        P("section", "dp", "tensor"),
        P("section", None),
        P(None, ("dp", "tensor"), None),
        P(),
        P(),
    )
    return jax.shard_map(
        shards,
        mesh=mesh,
        in_specs=placed,
        out_specs=(P("section", None, ("dp", "tensor"), None), P("section", "dp", "tensor")),
        check_vma=False,
    )
```
